32 devices in a mesh: path: 8 (over y, x, core), fac: 4 (over z).
Axes of the slice: x: 2, y: 2, z: 4, core: 2. Of those that a mesh axis runs over, the one named last changes fastest.
Arguments:
- shocks: bfloat16 [4, 512, 8192], P(None, 'path', 'fac'), may hold values from -6 to 6
- chol_factor: bfloat16 [8192, 8192], P('path', 'fac')
- factor_vol: float32 [8192], P('fac'), may hold values from 0.3 to 1.5
- trade_loading: bfloat16 [8192, 2048], P(None, 'fac'), may hold values from -0.0625 to 0.0625
- basis_loading: bfloat16 [8192, 64], replicated, may hold values from -0.0625 to 0.0625
- trade_set: int32 [2048], P('fac'), may hold values from 0 to 4095, as said below
Outputs:
- exposure: float32 [4, 512, 4096], P(None, 'path', 'fac')
The draws below stay inside these ranges and needn't reach their ends.
Inputs may be any that keep to these rules, and one draw needn't show every extreme that they name: Each trade belongs to a netting set of its own block: trade_set[k] // 1024 equals k // 512.
All inputs are finite; a program needn't handle non-finite values.
Results may differ from the reference program's by a relative error of at most 0.0047.
Values may be sent and summed in bfloat16 or wider, within the bound.
No kernel may reach another device: no remote copies, remote signals or barrier semaphores. Data moves between devices by JAX's collectives and lax.ppermute only.
A program may use at most 128 MiB of HBM per device.

```python
import math
import jax
import jax.numpy as jnp
from jax import lax

F = 8192
NSETS = 4096
NB = 64
STEPS = 4
TR_DEV = 512
PATHS = 512
TRADES = 2048
NS_DEV = 1024


def draw_chol_factor(key, part):
    row_index = lax.broadcasted_iota(jnp.int32, (F, F), 0)
    col_index = lax.broadcasted_iota(jnp.int32, (F, F), 1)
    noise = jax.random.normal(key, (F, F), jnp.float32)
    scale = 1.0 / jnp.sqrt(jnp.maximum(row_index, 1).astype(jnp.float32))
    lower = jnp.where(col_index < row_index, noise * scale, 0.0)
    return jnp.where(row_index == col_index, 1.0, lower).astype(jnp.bfloat16)


def draw_trade_set(key, part):
    trade_index = jnp.arange(TRADES, dtype=jnp.int32)
    block_index = trade_index // TR_DEV
    within = trade_index % TR_DEV
    local_set = jax.random.randint(key, (TRADES,), 0, NS_DEV, dtype=jnp.int32)
    local_set = jnp.where(within == 0, 0, jnp.where(within == 1, NS_DEV - 1, local_set))
    return (block_index * NS_DEV + local_set).astype(jnp.int32)


def block_levels(stream_key, shape, cuts, smallest, largest):
    level = 1.0
    for axis_at, parts in cuts:
        heights = jax.random.uniform(jax.random.fold_in(jax.random.fold_in(stream_key, 6), axis_at), (parts,), jnp.float32, smallest / len(cuts), largest / len(cuts))
        level = level * jnp.repeat(jnp.exp(heights), shape[axis_at] // parts).reshape((-1,) + (1,) * (len(shape) - 1 - axis_at))
    return level


def centred(rng, dims, deviation, limit, split=(), kind=jnp.bfloat16):
    entries = deviation * jax.random.normal(rng, dims, jnp.float32)
    if split:
        entries = entries * block_levels(rng, dims, split, -0.22, 0.18)
    return jnp.clip(entries, -limit, limit).astype(kind)


def setup_inputs(seed: int = 0) -> dict:
    seeds = jax.random.split(jax.random.key(seed), 7)
    shocks = centred(seeds[0], (STEPS, PATHS, F), 1.0, 6.0, ((1, 8), (2, 4)))
    chol_factor = draw_chol_factor(jax.random.fold_in(seeds[6], 71), 0)
    factor_vol = jnp.clip(jnp.exp(math.log(1.5) - 1.60943787 * jax.random.uniform(seeds[2], (F,), jnp.float32) ** block_levels(seeds[2], (F,), ((0, 4),), -0.2, 0.2)), 0.3, 1.5)
    trade_loading = centred(seeds[3], (F, TRADES), F ** -0.5, 0.0625, ((1, 4),))
    basis_loading = centred(seeds[4], (F, NB), F ** -0.5, 0.0625)
    trade_set = draw_trade_set(jax.random.fold_in(seeds[6], 71), 0)
    return {"shocks": shocks, "chol_factor": chol_factor, "factor_vol": factor_vol, "trade_loading": trade_loading, "basis_loading": basis_loading, "trade_set": trade_set}


def solve_step(gram, moment, basis, total_paths):
    ridged = gram + 0.01 * total_paths * jnp.eye(gram.shape[0], dtype=jnp.float32)
    factor = jnp.linalg.cholesky(ridged)
    coef = jax.scipy.linalg.cho_solve((factor, True), moment)
    predicted = jnp.dot(basis.astype(jnp.float32), coef.astype(jnp.float32), precision=lax.Precision.HIGHEST, preferred_element_type=jnp.float32)
    return jnp.maximum(predicted, 0.0)

def reference(shocks, chol_factor, factor_vol, trade_loading, basis_loading, trade_set):
    flat_shocks = shocks.reshape(STEPS * PATHS, F)
    increments = jnp.dot(flat_shocks.astype(jnp.float32), chol_factor.T.astype(jnp.float32), preferred_element_type=jnp.float32)
    scaled = increments.reshape(STEPS, PATHS, F) * (factor_vol / math.sqrt(STEPS))
    levels = jnp.cumsum(scaled, axis=0).astype(jnp.bfloat16).reshape(STEPS * PATHS, F)
    drivers = jnp.dot(levels.astype(jnp.float32), trade_loading.astype(jnp.float32), preferred_element_type=jnp.float32)
    projected = jnp.dot(levels.astype(jnp.float32), basis_loading.astype(jnp.float32), preferred_element_type=jnp.float32)
    values = jax.nn.softplus(drivers) - 1.0
    member = (trade_set[:, None] == jnp.arange(NSETS, dtype=jnp.int32)[None, :]).astype(jnp.float32)
    netting = jnp.dot(values.astype(jnp.float32), member.astype(jnp.float32), precision=lax.Precision.HIGHEST, preferred_element_type=jnp.float32)
    basis = jnp.tanh(projected).reshape(STEPS, PATHS, NB)
    netting = netting.reshape(STEPS, PATHS, NSETS)
    results = []
    for step in range(STEPS):
        step_basis = basis[step]
        gram = jnp.dot(step_basis.T.astype(jnp.float32), step_basis.astype(jnp.float32), precision=lax.Precision.HIGHEST, preferred_element_type=jnp.float32)
        moment = jnp.dot(step_basis.T.astype(jnp.float32), netting[step].astype(jnp.float32), precision=lax.Precision.HIGHEST, preferred_element_type=jnp.float32)
        results.append(solve_step(gram, moment, step_basis, PATHS))
    return jnp.stack(results)
```

```python
import math

import jax
import jax.numpy as jnp
from jax import lax
from jax.sharding import PartitionSpec as P

NSETS = 4096
HALVES = 2
HIGHEST = lax.Precision.HIGHEST
CONTRACT_LAST = (((1,), (1,)), ((), ()))


def flip_bits(blocks, own):
    count = blocks.shape[0]
    tail = blocks.shape[1:]
    bit = 1
    while bit < count:
        split = blocks.reshape(count // (2 * bit), 2, bit, *tail)
        swapped = split[:, ::-1]
        blocks = jnp.where((own & bit) != 0, swapped, split).reshape(count, *tail)
        bit *= 2
    return blocks


def sum_over_path(value, path_index, path_size):
    def exchange(x, k):
        return lax.ppermute(x, "path", [(i, i ^ k) for i in range(path_size)])

    core = path_index & 1
    steps, rows, columns = value.shape
    halves = value.reshape(steps, 2, rows // 2, columns)
    kept = lax.dynamic_index_in_dim(halves, core, axis=1, keepdims=False)
    given = lax.dynamic_index_in_dim(halves, 1 - core, axis=1, keepdims=False)
    total = kept + exchange(given, 1)
    bit = 2
    while bit < path_size:
        total = total + exchange(total, bit)
        bit *= 2
    other = exchange(total, 1)
    first = jnp.where(core == 0, total, other)
    second = jnp.where(core == 0, other, total)
    return jnp.concatenate([first, second], axis=1)


def on_device(shocks, chol_factor, factor_vol, trade_loading, basis_loading, trade_set):
    step_count, path_count, fac_width = shocks.shape
    row_block = chol_factor.shape[0]
    factor_count, trade_count = trade_loading.shape
    basis_count = basis_loading.shape[1]
    path_size, fac_size = lax.axis_size("path"), lax.axis_size("fac")
    path_index, fac_index = lax.axis_index("path"), lax.axis_index("fac")
    share = path_count // fac_size
    half_steps = step_count // HALVES
    chunk_rows = half_steps * share
    ring = [(i, (i + 1) % fac_size) for i in range(fac_size)]

    def exchange(x, k):
        return lax.ppermute(x, "path", [(i, i ^ k) for i in range(path_size)])

    def pass_on(x):
        return lax.ppermute(x, "fac", ring)

    row_peak = jnp.max(jnp.abs(chol_factor), axis=1).astype(jnp.float32)
    note = jnp.concatenate([factor_vol, row_peak])
    vol_owner = (path_index * row_block) // fac_width
    vol_block = jnp.zeros_like(factor_vol)
    for hop in range(fac_size):
        source = (fac_index - hop) % fac_size
        vol_block = jnp.where(source == vol_owner, note[:fac_width], vol_block)
        row_peak = jnp.maximum(row_peak, note[fac_width:])
        if hop < fac_size - 1:
            note = pass_on(note)
    vol = lax.dynamic_slice(vol_block, ((path_index * row_block) % fac_width,), (row_block,))
    peak = jnp.clip(row_peak, 1e-30, 1e37) * (6.0 * factor_count / 49152.0)
    shrink = 1.0 / peak
    vol = vol / math.sqrt(step_count)

    by_share = shocks.reshape(HALVES, half_steps, fac_size, share, fac_width)
    ordered = jnp.stack(
        [
            lax.dynamic_index_in_dim(by_share, (fac_index - 1 - s) % fac_size, axis=2, keepdims=False)
            for s in range(fac_size)
        ],
        axis=1,
    ).reshape(HALVES, fac_size * chunk_rows, fac_width)

    even = list(range(2, path_size, 2))
    carry = jnp.zeros((path_size, share, row_block), jnp.float32)
    local_set = trade_set % (NSETS // fac_size)
    sets_here = NSETS // fac_size
    member = (local_set[:, None] == jnp.arange(sets_here, dtype=jnp.int32)[None, :]).astype(
        jnp.float32
    )
    results = []
    for half in range(HALVES):
        own = ordered[half]
        groups = [[0], even] if half == 0 else [[0] + even]
        parts = []
        for group in groups:
            mine = jnp.stack([own if k == 0 else exchange(own, k) for k in group])
            sibling = exchange(mine, 1)
            sums = []
            for block in (mine, sibling):
                product = lax.dot_general(
                    block.reshape(-1, fac_width),
                    chol_factor,
                    CONTRACT_LAST,
                    preferred_element_type=jnp.float32,
                )
                sums.append((product * shrink).reshape(len(group), fac_size, chunk_rows, row_block))
            running = None
            for hop in range(fac_size):
                term = jnp.stack([s[:, hop] for s in sums], axis=1)
                if running is not None:
                    term = term + running.astype(jnp.float32)
                if hop < fac_size - 1:
                    running = pass_on(term.astype(jnp.float16))
            parts.append(term.reshape(2 * len(group), half_steps, share, row_block))
        increments = jnp.concatenate(parts, axis=0) * peak
        levels = []
        for step in range(half_steps):
            carry = carry + increments[:, step]
            levels.append((carry * vol).astype(jnp.bfloat16))
        levels = jnp.stack(levels, axis=1).reshape(path_size, chunk_rows, row_block)
        levels = flip_bits(levels, path_index)
        piece = lax.all_to_all(levels, "path", split_axis=0, concat_axis=0, tiled=True)
        pieces = [piece]
        for hop in range(fac_size - 1):
            piece = pass_on(piece)
            pieces.append(piece)
        all_levels = jnp.stack(pieces).transpose(0, 2, 1, 3).reshape(-1, factor_count)
        basis = jnp.tanh(jnp.dot(all_levels, basis_loading, preferred_element_type=jnp.float32))
        drivers = jnp.dot(all_levels, trade_loading, preferred_element_type=jnp.float32)
        values = jax.nn.softplus(drivers) - 1.0
        basis = basis.reshape(fac_size, half_steps, share, basis_count)
        joint = jnp.concatenate(
            [basis, values.reshape(fac_size, half_steps, share, trade_count)], axis=-1
        )
        sums = jnp.einsum(
            "ctpm,ctpn->tmn", basis, joint, precision=HIGHEST, preferred_element_type=jnp.float32
        )
        sums = sum_over_path(sums, path_index, path_size)
        gram, moment = sums[..., :basis_count], sums[..., basis_count:]
        ridge = 0.01 * path_count * path_size * jnp.eye(basis_count, dtype=jnp.float32)
        in_order = jnp.stack(
            [
                lax.dynamic_index_in_dim(basis, (fac_index - c) % fac_size, axis=0, keepdims=False)
                for c in range(fac_size)
            ],
            axis=1,
        ).reshape(half_steps, path_count, basis_count)
        for step in range(half_steps):
            factor = jnp.linalg.cholesky(gram[step] + ridge)
            coef = jax.scipy.linalg.cho_solve((factor, True), moment[step])
            by_trade = jnp.dot(
                in_order[step], coef, precision=HIGHEST, preferred_element_type=jnp.float32
            )
            predicted = jnp.dot(
                by_trade, member, precision=HIGHEST, preferred_element_type=jnp.float32
            )
            results.append(jnp.maximum(predicted, 0.0))
    return jnp.stack(results)


def solution(mesh):
    in_specs = (P(None, "path", "fac"), P("path", "fac"), P("fac"), P(None, "fac"), P(), P("fac"))
    out_specs = P(None, "path", "fac")
    return jax.shard_map(
        on_device, mesh=mesh, in_specs=in_specs, out_specs=out_specs, check_vma=False
    )
```

```python
import functools
import math

import jax
import jax.numpy as jnp
from jax import lax
from jax.experimental import pallas as pl
from jax.experimental.pallas import tpu as pltpu
from jax.sharding import PartitionSpec as P

NSETS = 4096
HALVES = 2
LANES = 128
VMEM_LIMIT = 24 * 2**20
HIGHEST = lax.Precision.HIGHEST
CONTRACT_LAST = (((1,), (1,)), ((), ()))
CONTRACT_FIRST = (((0,), (0,)), ((), ()))


def dot(a, b, dims, precision=None):
    return lax.dot_general(a, b, dims, precision=precision, preferred_element_type=jnp.float32)


def flip_bits(blocks, own):
    count = blocks.shape[0]
    tail = blocks.shape[1:]
    bit = 1
    while bit < count:
        split = blocks.reshape(count // (2 * bit), 2, bit, *tail)
        swapped = split[:, ::-1]
        blocks = jnp.where((own & bit) != 0, swapped, split).reshape(count, *tail)
        bit *= 2
    return blocks


def price_kernel(fac_size, place, *refs):
    pieces, (trade, basis_load, kept, given, ordered, driver_sum, basis_sum) = (
        refs[:fac_size],
        refs[fac_size:],
    )
    block = pl.program_id(0)

    @pl.when(block == 0)
    def _():
        driver_sum[...] = jnp.zeros_like(driver_sum)
        basis_sum[...] = jnp.zeros_like(basis_sum)

    levels = jnp.concatenate([piece[0] for piece in pieces], axis=0)
    driver_sum[...] += jnp.dot(levels, trade[...], preferred_element_type=jnp.float32)
    basis_sum[...] += dot(levels, basis_load[...], CONTRACT_LAST)

    @pl.when(block == pl.num_programs(0) - 1)
    def _():
        drivers = driver_sum[...]
        values = jnp.maximum(drivers, 0.0) + jnp.log1p(jnp.exp(-jnp.abs(drivers))) - 1.0
        basis = jnp.tanh(basis_sum[...])
        steps, paths, basis_count = ordered.shape
        share = paths // fac_size
        fac_index, core = place[0], place[1]
        sums = []
        for step in range(steps):
            rows = [
                slice((hop * steps + step) * share, (hop * steps + step + 1) * share)
                for hop in range(fac_size)
            ]
            for hop in range(fac_size):
                source = lax.rem(fac_index - hop + fac_size, fac_size)
                at = pl.multiple_of(source * share, share)
                ordered[step, pl.ds(at, share), :] = basis[rows[hop]]
            step_basis = jnp.concatenate([basis[r] for r in rows], axis=0)
            step_values = jnp.concatenate([values[r] for r in rows], axis=0)
            joint = jnp.concatenate([step_values, step_basis, step_basis], axis=1)
            sums.append(dot(step_basis, joint, CONTRACT_FIRST, HIGHEST))
        kept[...] = jnp.where(core == 0, sums[0], sums[1])
        given[...] = jnp.where(core == 0, sums[1], sums[0])


def price(pieces, trade_loading, basis_rows, place, steps, paths):
    fac_size = len(pieces)
    blocks, rows, width = pieces[0].shape
    trades, basis_count = trade_loading.shape[1], basis_rows.shape[0]
    columns = trades + 2 * basis_count
    sums = jax.ShapeDtypeStruct((basis_count, columns), jnp.float32)
    whole = pl.BlockSpec((basis_count, columns), lambda n: (0, 0))
    return pl.pallas_call(
        functools.partial(price_kernel, fac_size),
        grid=(blocks,),
        in_specs=[pl.BlockSpec(memory_space=pltpu.SMEM)]
        + [pl.BlockSpec((1, rows, width), lambda n: (n, 0, 0))] * fac_size
        + [
            pl.BlockSpec((width, trades), lambda n: (n, 0)),
            pl.BlockSpec((basis_count, width), lambda n: (0, n)),
        ],
        out_specs=[whole, whole, pl.BlockSpec((steps, paths, basis_count), lambda n: (0, 0, 0))],
        out_shape=[sums, sums, jax.ShapeDtypeStruct((steps, paths, basis_count), jnp.float32)],
        scratch_shapes=[
            pltpu.VMEM((fac_size * rows, trades), jnp.float32),
            pltpu.VMEM((fac_size * rows, basis_count), jnp.float32),
        ],
        compiler_params=pltpu.CompilerParams(vmem_limit_bytes=VMEM_LIMIT),
        cost_estimate=pl.CostEstimate(
            flops=2 * fac_size * rows * blocks * width * (trades + basis_count),
            bytes_accessed=2 * blocks * width * (trades + fac_size * rows),
            transcendentals=2 * fac_size * rows * trades,
        ),
        name="price",
    )(place, *pieces, trade_loading, basis_rows)


def solve_kernel(ridge, first, second, coef):
    count, trades = coef.shape
    sums = first[...] + second[...]
    row = lax.broadcasted_iota(jnp.int32, (count, 2 * count), 0)
    lane = lax.broadcasted_iota(jnp.int32, (count, 2 * count), 1)
    work = jnp.where(lane < count, sums[:, trades:], 0.0)
    work = work + jnp.where(lane == row, ridge, 0.0) + jnp.where(lane == row + count, 1.0, 0.0)
    for j in range(count):
        scaled = work[j : j + 1, :] / work[j : j + 1, j : j + 1]
        work = jnp.where(row == j, scaled, work - work[:, j : j + 1] * scaled)
    coef[...] = jnp.dot(
        work[:, count:], sums[:, :trades], precision=HIGHEST, preferred_element_type=jnp.float32
    )


def solve(first, second, trades, ridge):
    count = first.shape[0]
    return pl.pallas_call(
        functools.partial(solve_kernel, ridge),
        out_shape=jax.ShapeDtypeStruct((count, trades), jnp.float32),
        compiler_params=pltpu.CompilerParams(vmem_limit_bytes=VMEM_LIMIT),
        cost_estimate=pl.CostEstimate(
            flops=2 * count**3 + 12 * count * count * trades,
            bytes_accessed=4 * count * trades * 3,
            transcendentals=0,
        ),
        name="solve",
    )(first, second)


def expose_kernel(place, basis, mine, other, local_set, out):
    core = place[1]
    trades = mine.shape[1]
    sets = out.shape[2]
    member = jnp.where(
        lax.broadcasted_iota(jnp.int32, (sets, trades), 0) == local_set[...], 1.0, 0.0
    )
    for step in range(out.shape[0]):
        coef = jnp.where(core == step, mine[...], other[...])
        by_trade = jnp.dot(
            basis[step], coef, precision=HIGHEST, preferred_element_type=jnp.float32
        )
        out[step] = jnp.maximum(dot(by_trade, member, CONTRACT_LAST, HIGHEST), 0.0)


def expose(place, basis, mine, other, local_set, sets):
    steps, paths, _ = basis.shape
    trades = mine.shape[1]
    vmem = pl.BlockSpec(memory_space=pltpu.VMEM)
    return pl.pallas_call(
        expose_kernel,
        in_specs=[pl.BlockSpec(memory_space=pltpu.SMEM)] + [vmem] * 4,
        out_specs=vmem,
        out_shape=jax.ShapeDtypeStruct((steps, paths, sets), jnp.float32),
        compiler_params=pltpu.CompilerParams(vmem_limit_bytes=VMEM_LIMIT),
        cost_estimate=pl.CostEstimate(
            flops=12 * steps * paths * trades * sets,
            bytes_accessed=4 * steps * paths * sets * 2,
            transcendentals=0,
        ),
        name="expose",
    )(place, basis, mine, other, local_set)


def on_device(shocks, chol_factor, factor_vol, trade_loading, basis_loading, trade_set):
    step_count, path_count, fac_width = shocks.shape
    row_block = chol_factor.shape[0]
    factor_count, trade_count = trade_loading.shape
    path_size, fac_size = lax.axis_size("path"), lax.axis_size("fac")
    path_index, fac_index = lax.axis_index("path"), lax.axis_index("fac")
    share = path_count // fac_size
    half_steps = step_count // HALVES
    chunk_rows = half_steps * share
    place = jnp.stack([fac_index, path_index & 1]).astype(jnp.int32)

    def exchange(x, k):
        return lax.ppermute(x, "path", [(i, i ^ k) for i in range(path_size)])

    def pass_on(x, hops=1):
        return lax.ppermute(x, "fac", [(i, (i + hops) % fac_size) for i in range(fac_size)])

    by_share = shocks.reshape(HALVES, half_steps, fac_size, share, fac_width)
    ordered = jnp.stack(
        [
            lax.dynamic_index_in_dim(by_share, (fac_index - 1 - s) % fac_size, axis=2, keepdims=False)
            for s in range(fac_size)
        ],
        axis=1,
    ).reshape(HALVES, fac_size * chunk_rows, fac_width)

    even = list(range(2, path_size, 2))
    gathered = []
    own = ordered[0]
    for half in range(HALVES):
        received = [exchange(own, k) for k in even]
        rest = jnp.stack(received)
        near = jnp.stack([own, exchange(own, 1)])
        gathered.append((near, rest, exchange(rest, 1)))
        if half + 1 < HALVES:
            own, _ = lax.optimization_barrier((ordered[half + 1], received))

    row_peak = jnp.max(jnp.abs(chol_factor), axis=1).astype(jnp.float32)
    note = jnp.concatenate([factor_vol, row_peak])
    vol_owner = (path_index * row_block) // fac_width
    vol_block = jnp.zeros_like(factor_vol)
    for hops in range(fac_size):
        arrived = note if hops == 0 else pass_on(note, hops)
        source = (fac_index - hops) % fac_size
        vol_block = jnp.where(source == vol_owner, arrived[:fac_width], vol_block)
        row_peak = jnp.maximum(row_peak, arrived[fac_width:])
    vol = lax.dynamic_slice(vol_block, ((path_index * row_block) % fac_width,), (row_block,))
    peak = jnp.clip(row_peak, 1e-30, 1e37) * (6.0 * factor_count / 49152.0)
    shrink = 1.0 / peak
    vol = vol / math.sqrt(step_count)

    carry = jnp.zeros((path_size, share, row_block), jnp.float32)
    sets_here = NSETS // fac_size
    local_set = (trade_set % sets_here)[None, :]
    basis_rows = basis_loading.T
    ridge = 0.01 * path_count * path_size

    def partial_sums(block):
        product = dot(block.reshape(-1, fac_width), chol_factor, CONTRACT_LAST)
        return (product * shrink).reshape(block.shape[0], fac_size, chunk_rows, row_block)

    def reduce_over_fac(terms):
        running = None
        for hop in range(fac_size):
            term = jnp.concatenate([t[:, hop] for t in terms], axis=0)
            if running is not None:
                term = term + running.astype(jnp.float32)
            if hop < fac_size - 1:
                running = pass_on(term.astype(jnp.float16))
        return term.reshape(-1, half_steps, share, row_block)

    results = []
    for half in range(HALVES):
        near, rest, rest_sibling = gathered[half]
        near = partial_sums(near)
        rest, rest_sibling = partial_sums(rest), partial_sums(rest_sibling)
        if half == 0:
            near_sum, rest_sum = reduce_over_fac([near]), reduce_over_fac([rest, rest_sibling])
        else:
            total = reduce_over_fac([near, rest, rest_sibling])
            near_sum, rest_sum = total[:2], total[2:]
        far = len(even)
        increments = jnp.stack(
            [
                jnp.concatenate([near_sum[:1], rest_sum[:far]]),
                jnp.concatenate([near_sum[1:], rest_sum[far:]]),
            ],
            axis=1,
        ).reshape(path_size, half_steps, share, row_block)
        increments = increments * peak
        levels = []
        for step in range(half_steps):
            carry = carry + increments[:, step]
            levels.append((carry * vol).astype(jnp.bfloat16))
        levels = jnp.stack(levels, axis=1).reshape(path_size, chunk_rows, row_block)
        levels = flip_bits(levels, path_index)
        piece = lax.all_to_all(levels, "path", split_axis=0, concat_axis=0, tiled=True)
        pieces = [piece]
        for hop in range(fac_size - 1):
            piece = pass_on(piece)
            pieces.append(piece)
        kept, given, basis = price(pieces, trade_loading, basis_rows, place, half_steps, path_count)
        total = kept + exchange(given, 1)
        bit = 2
        while 2 * bit < path_size:
            total = total + exchange(total, bit)
            bit *= 2
        coef = solve(total, exchange(total, bit), trade_count, ridge)
        results.append(expose(place, basis, coef, exchange(coef, 1), local_set, sets_here))
    return jnp.concatenate(results, axis=0)


def solution(mesh):
    in_specs = (P(None, "path", "fac"), P("path", "fac"), P("fac"), P(None, "fac"), P(), P("fac"))
    out_specs = P(None, "path", "fac")
    return jax.shard_map(
        on_device, mesh=mesh, in_specs=in_specs, out_specs=out_specs, check_vma=False
    )
```

```python
import functools
import math

import jax
import jax.numpy as jnp
from jax import lax
from jax.experimental import pallas as pl
from jax.experimental.pallas import tpu as pltpu
from jax.sharding import PartitionSpec as P

NSETS = 4096
HALVES = 2
VMEM_LIMIT = 24 * 2**20
HIGHEST = lax.Precision.HIGHEST
CONTRACT_LAST = (((1,), (1,)), ((), ()))
CONTRACT_FIRST = (((0,), (0,)), ((), ()))


def dot(a, b, dims, precision=None):
    return lax.dot_general(a, b, dims, precision=precision, preferred_element_type=jnp.float32)


def price_kernel(place, *refs):
    trade, basis_load, kept, given, ordered = refs[-5:]
    pieces = refs[:-5]
    fac_size = len(pieces)
    blocks, rows, _ = pieces[0].shape
    drivers = jnp.zeros((fac_size * rows, trade.shape[2]), jnp.float32)
    projected = jnp.zeros((fac_size * rows, basis_load.shape[1]), jnp.float32)
    for n in range(blocks):
        levels = jnp.concatenate([piece[n] for piece in pieces], axis=0)
        factors = place[2 + n]
        drivers += jnp.dot(levels, trade[factors], preferred_element_type=jnp.float32)
        projected += dot(levels, basis_load[factors], CONTRACT_LAST)
    values = jnp.maximum(drivers, 0.0) + jnp.log1p(jnp.exp(-jnp.abs(drivers))) - 1.0
    basis = jnp.tanh(projected)
    steps, paths, basis_count = ordered.shape
    share = paths // fac_size
    fac_index, core = place[0], place[1]
    sums = []
    for step in range(steps):
        spans = [
            slice((hop * steps + step) * share, (hop * steps + step + 1) * share)
            for hop in range(fac_size)
        ]
        for hop in range(fac_size):
            source = lax.rem(fac_index - hop + fac_size, fac_size)
            at = pl.multiple_of(source * share, share)
            ordered[step, pl.ds(at, share), :] = basis[spans[hop]]
        step_basis = jnp.concatenate([basis[s] for s in spans], axis=0)
        step_values = jnp.concatenate([values[s] for s in spans], axis=0)
        joint = jnp.concatenate([step_values, step_basis, step_basis], axis=1)
        sums.append(dot(step_basis, joint, CONTRACT_FIRST, HIGHEST))
    kept[...] = jnp.where(core == 0, sums[0], sums[1])
    given[...] = jnp.where(core == 0, sums[1], sums[0])


def price(pieces, trade_blocks, basis_blocks, place, steps, paths):
    fac_size = len(pieces)
    blocks, rows, width = pieces[0].shape
    trades, basis_count = trade_blocks.shape[2], basis_blocks.shape[1]
    sums = jax.ShapeDtypeStruct((basis_count, trades + 2 * basis_count), jnp.float32)
    vmem = pl.BlockSpec(memory_space=pltpu.VMEM)
    return pl.pallas_call(
        price_kernel,
        in_specs=[pl.BlockSpec(memory_space=pltpu.SMEM)] + [vmem] * (fac_size + 2),
        out_specs=[vmem] * 3,
        out_shape=[sums, sums, jax.ShapeDtypeStruct((steps, paths, basis_count), jnp.float32)],
        compiler_params=pltpu.CompilerParams(vmem_limit_bytes=VMEM_LIMIT),
        cost_estimate=pl.CostEstimate(
            flops=2 * fac_size * rows * blocks * width * (trades + basis_count),
            bytes_accessed=2 * blocks * width * (trades + fac_size * rows),
            transcendentals=2 * fac_size * rows * trades,
        ),
        name="price",
    )(place, *pieces, trade_blocks, basis_blocks)


def solve_kernel(ridge, first_top, first_bottom, second_top, second_bottom, coef):
    count, trades = coef.shape
    sums = jnp.concatenate(
        [first_top[...] + second_top[...], first_bottom[...] + second_bottom[...]], axis=0
    )
    row = lax.broadcasted_iota(jnp.int32, (count, 2 * count), 0)
    lane = lax.broadcasted_iota(jnp.int32, (count, 2 * count), 1)
    work = jnp.where(lane < count, sums[:, trades:], 0.0)
    work = work + jnp.where(lane == row, ridge, 0.0) + jnp.where(lane == row + count, 1.0, 0.0)
    for j in range(0, count, 2):
        left = jnp.broadcast_to(work[:, j : j + 1], work.shape)
        right = jnp.broadcast_to(work[:, j + 1 : j + 2], work.shape)
        upper, lower = work[j : j + 1, :], work[j + 1 : j + 2, :]
        a, b = left[j : j + 1, :], right[j : j + 1, :]
        c, d = left[j + 1 : j + 2, :], right[j + 1 : j + 2, :]
        scale = 1.0 / (a * d - b * c)
        new_upper = (d * upper - b * lower) * scale
        new_lower = (a * lower - c * upper) * scale
        work = work - left * new_upper - right * new_lower
        work = jnp.where(row == j, new_upper, jnp.where(row == j + 1, new_lower, work))
    coef[...] = jnp.dot(
        work[:, count:], sums[:, :trades], precision=HIGHEST, preferred_element_type=jnp.float32
    )


def solve(parts, trades, ridge):
    count = 2 * parts[0].shape[0]
    return pl.pallas_call(
        functools.partial(solve_kernel, ridge),
        out_shape=jax.ShapeDtypeStruct((count, trades), jnp.float32),
        compiler_params=pltpu.CompilerParams(vmem_limit_bytes=VMEM_LIMIT),
        cost_estimate=pl.CostEstimate(
            flops=2 * count**3 + 12 * count * count * trades,
            bytes_accessed=4 * count * trades * 3,
            transcendentals=0,
        ),
        name="solve",
    )(*parts)


def expose_kernel(place, basis, mine, other, member, *refs):
    out = refs[-1]
    core = place[1]
    steps, paths, sets = out.shape
    by_trade = jnp.concatenate(
        [
            jnp.dot(
                basis[step],
                jnp.where(core == step, mine[...], other[...]),
                precision=HIGHEST,
                preferred_element_type=jnp.float32,
            )
            for step in range(steps)
        ],
        axis=0,
    )
    terms = []
    for _ in range(3):
        term = by_trade.astype(jnp.bfloat16)
        by_trade = by_trade - term.astype(jnp.float32)
        terms.append(term)
    spread = [jnp.dot(t, member[...], preferred_element_type=jnp.float32) for t in terms]
    total = jnp.maximum(spread[0] + (spread[1] + spread[2]), 0.0)
    for step in range(steps):
        out[step] = total[step * paths : (step + 1) * paths]


def expose(place, basis, mine, other, member, half, so_far):
    steps, paths, _ = basis.shape
    trades, sets = member.shape
    vmem = pl.BlockSpec(memory_space=pltpu.VMEM)
    block = pl.BlockSpec((steps, paths, sets), lambda i: (half, 0, 0))
    earlier = [] if so_far is None else [so_far]
    return pl.pallas_call(
        expose_kernel,
        grid=(1,),
        in_specs=[pl.BlockSpec(memory_space=pltpu.SMEM)]
        + [vmem] * 4
        + [pl.BlockSpec(memory_space=pl.ANY)] * len(earlier),
        out_specs=block,
        out_shape=jax.ShapeDtypeStruct((HALVES * steps, paths, sets), jnp.float32),
        input_output_aliases={5: 0} if earlier else {},
        compiler_params=pltpu.CompilerParams(vmem_limit_bytes=VMEM_LIMIT),
        cost_estimate=pl.CostEstimate(
            flops=6 * steps * paths * trades * sets,
            bytes_accessed=4 * steps * paths * sets * 2,
            transcendentals=0,
        ),
        name="expose",
    )(place, basis, mine, other, member, *earlier)


def on_device(shocks, chol_factor, factor_vol, trade_loading, basis_loading, trade_set):
    step_count, path_count, fac_width = shocks.shape
    row_block = chol_factor.shape[0]
    factor_count, trade_count = trade_loading.shape
    path_size, fac_size = lax.axis_size("path"), lax.axis_size("fac")
    path_index, fac_index = lax.axis_index("path"), lax.axis_index("fac")
    share = path_count // fac_size
    half_steps = step_count // HALVES
    chunk_rows = half_steps * share
    sets_here = NSETS // fac_size
    ridge = 0.01 * path_count * path_size
    even = list(range(2, path_size, 2))
    bits = [2**n for n in range(1, path_size.bit_length() - 1)]
    place = jnp.concatenate(
        [
            jnp.stack([fac_index, path_index & 1]),
            path_index ^ jnp.arange(path_size, dtype=jnp.int32),
        ]
    ).astype(jnp.int32)

    def exchange(x, k):
        return lax.ppermute(x, "path", [(i, i ^ k) for i in range(path_size)])

    def pass_on(x, hops=1):
        return lax.ppermute(x, "fac", [(i, (i + hops) % fac_size) for i in range(fac_size)])

    last = []

    def gate(*values):
        held = lax.optimization_barrier((values, tuple(last)))[0]
        return held[0] if len(held) == 1 else held

    def mark(*values):
        last[:] = values
        return values[0]

    def partial_sums(block, scale):
        product = dot(block.reshape(-1, fac_width), chol_factor, CONTRACT_LAST)
        if scale is not None:
            product = product * scale
        return product.reshape(block.shape[0], fac_size, chunk_rows, row_block)

    def reduce_over_fac(block, scale, kind):
        terms = partial_sums(gate(block), scale)
        running = None
        for hop in range(fac_size):
            term = terms[:, hop]
            if running is not None:
                term = term + gate(running).astype(jnp.float32)
            if hop < fac_size - 1:
                running = pass_on(mark(term.astype(kind)))
                yield None
        yield mark(term).reshape(-1, half_steps, share, row_block)

    def gather_over_fac(piece):
        pieces = [mark(piece)]
        for _ in range(fac_size - 1):
            pieces.append(pass_on(pieces[-1]))
            yield None
            pieces[-1] = mark(gate(pieces[-1]))
        yield pieces

    by_share = shocks.reshape(HALVES, half_steps, fac_size, share, fac_width)
    ordered = jnp.stack(
        [
            lax.dynamic_index_in_dim(by_share, (fac_index - 1 - s) % fac_size, axis=2, keepdims=False)
            for s in range(fac_size)
        ],
        axis=1,
    ).reshape(HALVES, fac_size * chunk_rows, fac_width)

    own = mark(ordered[0])
    received = [exchange(own, k) for k in even]
    chain_a = reduce_over_fac(jnp.stack([own, exchange(own, 1)]), None, jnp.float32)
    next(chain_a)

    row_peak = jnp.max(jnp.abs(chol_factor), axis=1).astype(jnp.float32)
    vols, note = gate(factor_vol), None
    bit = 1
    while bit < fac_size:
        note = mark(jnp.concatenate([vols, row_peak]))
        swap = [(i, i ^ bit) for i in range(fac_size)]
        arrived = lax.ppermute(note, "fac", swap)
        next(chain_a)
        arrived = gate(arrived)
        split = arrived.shape[0] - row_block
        lower = (fac_index & bit) == 0
        vols = jnp.where(
            lower,
            jnp.concatenate([vols, arrived[:split]]),
            jnp.concatenate([arrived[:split], vols]),
        )
        row_peak = jnp.maximum(row_peak, arrived[split:])
        bit *= 2
    vol = lax.dynamic_slice(vols, (path_index * row_block,), (row_block,)) / math.sqrt(step_count)
    peak = jnp.clip(row_peak, 1e-30, 1e37) * (6.0 * factor_count / 49152.0)
    shrink = 1.0 / peak
    mark(shrink)

    trade_blocks = trade_loading.reshape(path_size, row_block, trade_count)
    basis_blocks = basis_loading.T.reshape(-1, path_size, row_block).transpose(1, 0, 2)
    local_set = trade_set % sets_here
    member = (local_set[:, None] == jnp.arange(sets_here, dtype=jnp.int32)[None, :]).astype(
        jnp.bfloat16
    )

    def levels_of(increments, carry):
        levels = []
        for step in range(half_steps):
            carry = carry + increments[:, step]
            levels.append((carry * vol).astype(jnp.bfloat16))
        return jnp.stack(levels, axis=1).reshape(-1, chunk_rows, row_block), carry

    def regroup(mine, others):
        arrived = exchange(mark(others), 1)
        yield None
        pairs = mark(jnp.stack([mine, gate(arrived)], axis=1))
        pairs = [pairs[0]] + [exchange(pairs[k // 2], k) for k in even]
        yield None
        yield jnp.concatenate(gate(*pairs), axis=0)

    def priced(pieces):
        kept, given, basis = price(pieces, trade_blocks, basis_blocks, place, half_steps, path_count)
        mark(given)
        return kept, given, basis

    def finish(kept, given, basis, half):
        arrived = exchange(given, 1)
        yield None
        total = mark(kept + gate(arrived))
        rows = total.shape[0] // 2
        top, bottom = total[:rows], total[rows:]
        for n, bit in enumerate(bits):
            more = exchange(top, bit), exchange(bottom, bits[-1 - n])
            yield None
            more = gate(*more)
            if n < len(bits) - 1:
                top, bottom = top + more[0], bottom + more[1]
                mark(top, bottom)
        coef = mark(solve((top, bottom, *more), trade_count, ridge))
        other = exchange(coef, 1)
        so_far = yield None
        yield mark(expose(place, basis, coef, gate(other), member, half, so_far))

    for _ in range(fac_size - 2 - (fac_size.bit_length() - 1)):
        next(chain_a)
    rest = mark(jnp.stack(gate(*received)))
    arrived = exchange(rest, 1)
    own = gate(ordered[1])
    received = [exchange(own, k) for k in even]
    chain_b = reduce_over_fac(rest, shrink, jnp.float16)
    next(chain_b)
    near_sum = next(chain_a)
    chain_c = reduce_over_fac(arrived, shrink, jnp.float16)
    next(chain_c)
    for hop in range(1, fac_size - 1):
        next(chain_b)
        next(chain_c)
    block = mark(jnp.stack([own, *gate(*received)]))
    arrived = exchange(block, 1)
    chain_d = reduce_over_fac(block, shrink, jnp.float16)
    next(chain_d)
    mine = jnp.concatenate([near_sum[:1], next(chain_b) * peak])
    mine, carry = levels_of(mine, 0.0)
    others = jnp.concatenate([near_sum[1:], next(chain_c) * peak])
    others, other_carry = levels_of(others, 0.0)
    first = regroup(mine, others)
    next(first)
    chain_e = reduce_over_fac(arrived, shrink, jnp.float16)
    next(chain_e)
    next(first)
    next(chain_d)
    next(chain_e)
    ring_first = gather_over_fac(next(first))
    next(ring_first)
    for hop in range(2, fac_size - 1):
        next(chain_d)
        next(chain_e)
    mine, _ = levels_of(next(chain_d) * peak, carry)
    others, _ = levels_of(next(chain_e) * peak, other_carry)
    second = regroup(mine, others)
    next(second)
    next(ring_first)
    next(second)
    for hop in range(2, fac_size - 1):
        next(ring_first)
    ring_second = gather_over_fac(next(second))
    next(ring_second)
    first = finish(*priced(next(ring_first)), 0)
    next(first)
    to_do = len(bits)
    for hop in range(1, fac_size - 1):
        next(ring_second)
        if to_do > 0:
            next(first)
            to_do -= 1
    for _ in range(to_do):
        next(first)
    second = finish(*priced(next(ring_second)), 1)
    next(second)
    next(second)
    next(first)
    for _ in range(len(bits) - 1):
        next(second)
    result = next(first)
    next(second)
    return second.send(result)


def solution(mesh):
    in_specs = (P(None, "path", "fac"), P("path", "fac"), P("fac"), P(None, "fac"), P(), P("fac"))
    out_specs = P(None, "path", "fac")
    return jax.shard_map(
        on_device, mesh=mesh, in_specs=in_specs, out_specs=out_specs, check_vma=False
    )
```

```python
import functools
import math

import jax
import jax.numpy as jnp
from jax import lax
from jax.experimental import pallas as pl
from jax.experimental.pallas import tpu as pltpu
from jax.sharding import PartitionSpec as P

NSETS = 4096
HALVES = 2
VMEM_LIMIT = 24 * 2**20
HIGHEST = lax.Precision.HIGHEST
CONTRACT_LAST = (((1,), (1,)), ((), ()))
CONTRACT_FIRST = (((0,), (0,)), ((), ()))


def dot(a, b, dims, precision=None):
    return lax.dot_general(a, b, dims, precision=precision, preferred_element_type=jnp.float32)


def accumulate(place, pieces, trade, basis_load):
    fac_parts = len(pieces)
    blocks, rows, _ = pieces[0].shape
    drivers = jnp.zeros((fac_parts * rows, trade.shape[2]), jnp.float32)
    projected = jnp.zeros((fac_parts * rows, basis_load.shape[1]), jnp.float32)
    for n in range(blocks):
        levels = jnp.concatenate([piece[n] for piece in pieces], axis=0)
        factors = place[2 + n]
        drivers += jnp.dot(levels, trade[factors], preferred_element_type=jnp.float32)
        projected += dot(levels, basis_load[factors], CONTRACT_LAST)
    return drivers, projected


def start_price_kernel(place, *refs):
    trade, basis_load, drivers, projected = refs[-4:]
    drivers[...], projected[...] = accumulate(place, refs[:-4], trade, basis_load)


def price_kernel(place, piece, trade, basis_load, drivers, projected, kept, given, ordered):
    rows = piece.shape[1]
    fac_size = drivers.shape[0] // rows + 1
    last_drivers, last_projected = accumulate(place, [piece], trade, basis_load)
    drivers = jnp.concatenate([drivers[...], last_drivers], axis=0)
    values = jnp.maximum(drivers, 0.0) + jnp.log1p(jnp.exp(-jnp.abs(drivers))) - 1.0
    basis = jnp.tanh(jnp.concatenate([projected[...], last_projected], axis=0))
    steps, paths, basis_count = ordered.shape
    share = paths // fac_size
    fac_index, core = place[0], place[1]
    sums = []
    for step in range(steps):
        spans = [
            slice((hop * steps + step) * share, (hop * steps + step + 1) * share)
            for hop in range(fac_size)
        ]
        for hop in range(fac_size):
            source = lax.rem(fac_index - hop + fac_size, fac_size)
            at = pl.multiple_of(source * share, share)
            ordered[step, pl.ds(at, share), :] = basis[spans[hop]]
        step_basis = jnp.concatenate([basis[s] for s in spans], axis=0)
        step_values = jnp.concatenate([values[s] for s in spans], axis=0)
        joint = jnp.concatenate([step_values, step_basis, step_basis], axis=1)
        sums.append(dot(step_basis, joint, CONTRACT_FIRST, HIGHEST))
    kept[...] = jnp.where(core == 0, sums[0], sums[1])
    given[...] = jnp.where(core == 0, sums[1], sums[0])


def start_price(pieces, trade_blocks, basis_blocks, place):
    blocks, rows, width = pieces[0].shape
    rows = len(pieces) * rows
    trades, basis_count = trade_blocks.shape[2], basis_blocks.shape[1]
    vmem = pl.BlockSpec(memory_space=pltpu.VMEM)
    return pl.pallas_call(
        start_price_kernel,
        in_specs=[pl.BlockSpec(memory_space=pltpu.SMEM)] + [vmem] * (len(pieces) + 2),
        out_specs=[vmem] * 2,
        out_shape=[
            jax.ShapeDtypeStruct((rows, trades), jnp.float32),
            jax.ShapeDtypeStruct((rows, basis_count), jnp.float32),
        ],
        compiler_params=pltpu.CompilerParams(vmem_limit_bytes=VMEM_LIMIT),
        cost_estimate=pl.CostEstimate(
            flops=2 * rows * blocks * width * (trades + basis_count),
            bytes_accessed=2 * blocks * width * (trades + rows),
            transcendentals=0,
        ),
        name="start_price",
    )(place, *pieces, trade_blocks, basis_blocks)


def price(piece, trade_blocks, basis_blocks, started, place, steps, paths):
    blocks, rows, width = piece.shape
    trades, basis_count = trade_blocks.shape[2], basis_blocks.shape[1]
    sums = jax.ShapeDtypeStruct((basis_count, trades + 2 * basis_count), jnp.float32)
    vmem = pl.BlockSpec(memory_space=pltpu.VMEM)
    return pl.pallas_call(
        price_kernel,
        in_specs=[pl.BlockSpec(memory_space=pltpu.SMEM)] + [vmem] * 5,
        out_specs=[vmem] * 3,
        out_shape=[sums, sums, jax.ShapeDtypeStruct((steps, paths, basis_count), jnp.float32)],
        compiler_params=pltpu.CompilerParams(vmem_limit_bytes=VMEM_LIMIT),
        cost_estimate=pl.CostEstimate(
            flops=2 * rows * blocks * width * (trades + basis_count),
            bytes_accessed=2 * blocks * width * (trades + rows),
            transcendentals=2 * steps * paths * trades,
        ),
        name="price",
    )(place, piece, trade_blocks, basis_blocks, *started)


def solve_kernel(ridge, first_top, first_bottom, second_top, second_bottom, coef):
    count, trades = coef.shape
    sums = jnp.concatenate(
        [first_top[...] + second_top[...], first_bottom[...] + second_bottom[...]], axis=0
    )
    row = lax.broadcasted_iota(jnp.int32, (count, 2 * count), 0)
    lane = lax.broadcasted_iota(jnp.int32, (count, 2 * count), 1)
    work = jnp.where(lane < count, sums[:, trades:], 0.0)
    work = work + jnp.where(lane == row, ridge, 0.0) + jnp.where(lane == row + count, 1.0, 0.0)
    for j in range(0, count, 2):
        left = jnp.broadcast_to(work[:, j : j + 1], work.shape)
        right = jnp.broadcast_to(work[:, j + 1 : j + 2], work.shape)
        upper, lower = work[j : j + 1, :], work[j + 1 : j + 2, :]
        a, b = left[j : j + 1, :], right[j : j + 1, :]
        c, d = left[j + 1 : j + 2, :], right[j + 1 : j + 2, :]
        scale = 1.0 / (a * d - b * c)
        new_upper = (d * upper - b * lower) * scale
        new_lower = (a * lower - c * upper) * scale
        work = work - left * new_upper - right * new_lower
        work = jnp.where(row == j, new_upper, jnp.where(row == j + 1, new_lower, work))
    coef[...] = jnp.dot(
        work[:, count:], sums[:, :trades], precision=HIGHEST, preferred_element_type=jnp.float32
    )


def solve(parts, trades, ridge):
    count = 2 * parts[0].shape[0]
    return pl.pallas_call(
        functools.partial(solve_kernel, ridge),
        out_shape=jax.ShapeDtypeStruct((count, trades), jnp.float32),
        compiler_params=pltpu.CompilerParams(vmem_limit_bytes=VMEM_LIMIT),
        cost_estimate=pl.CostEstimate(
            flops=2 * count**3 + 12 * count * count * trades,
            bytes_accessed=4 * count * trades * 3,
            transcendentals=0,
        ),
        name="solve",
    )(*parts)


def expose_kernel(place, basis, mine, other, member, *refs):
    out = refs[-1]
    core = place[1]
    steps, paths, sets = out.shape
    by_trade = jnp.concatenate(
        [
            jnp.dot(
                basis[step],
                jnp.where(core == step, mine[...], other[...]),
                precision=HIGHEST,
                preferred_element_type=jnp.float32,
            )
            for step in range(steps)
        ],
        axis=0,
    )
    terms = []
    for _ in range(3):
        term = by_trade.astype(jnp.bfloat16)
        by_trade = by_trade - term.astype(jnp.float32)
        terms.append(term)
    spread = [jnp.dot(t, member[...], preferred_element_type=jnp.float32) for t in terms]
    total = jnp.maximum(spread[0] + (spread[1] + spread[2]), 0.0)
    for step in range(steps):
        out[step] = total[step * paths : (step + 1) * paths]


def expose(place, basis, mine, other, member, half, so_far):
    steps, paths, _ = basis.shape
    trades, sets = member.shape
    vmem = pl.BlockSpec(memory_space=pltpu.VMEM)
    block = pl.BlockSpec((steps, paths, sets), lambda i: (half, 0, 0))
    earlier = [] if so_far is None else [so_far]
    return pl.pallas_call(
        expose_kernel,
        grid=(1,),
        in_specs=[pl.BlockSpec(memory_space=pltpu.SMEM)]
        + [vmem] * 4
        + [pl.BlockSpec(memory_space=pl.ANY)] * len(earlier),
        out_specs=block,
        out_shape=jax.ShapeDtypeStruct((HALVES * steps, paths, sets), jnp.float32),
        input_output_aliases={5: 0} if earlier else {},
        compiler_params=pltpu.CompilerParams(vmem_limit_bytes=VMEM_LIMIT),
        cost_estimate=pl.CostEstimate(
            flops=6 * steps * paths * trades * sets,
            bytes_accessed=4 * steps * paths * sets * 2,
            transcendentals=0,
        ),
        name="expose",
    )(place, basis, mine, other, member, *earlier)


def on_device(shocks, chol_factor, factor_vol, trade_loading, basis_loading, trade_set):
    step_count, path_count, fac_width = shocks.shape
    row_block = chol_factor.shape[0]
    factor_count, trade_count = trade_loading.shape
    path_size, fac_size = lax.axis_size("path"), lax.axis_size("fac")
    path_index, fac_index = lax.axis_index("path"), lax.axis_index("fac")
    share = path_count // fac_size
    half_steps = step_count // HALVES
    chunk_rows = half_steps * share
    sets_here = NSETS // fac_size
    ridge = 0.01 * path_count * path_size
    even = list(range(2, path_size, 2))
    bits = [2**n for n in range(1, path_size.bit_length() - 1)]
    place = jnp.concatenate(
        [
            jnp.stack([fac_index, path_index & 1]),
            path_index ^ jnp.arange(path_size, dtype=jnp.int32),
        ]
    ).astype(jnp.int32)

    def exchange(x, k):
        return lax.ppermute(x, "path", [(i, i ^ k) for i in range(path_size)])

    def pass_on(x, hops=1):
        return lax.ppermute(x, "fac", [(i, (i + hops) % fac_size) for i in range(fac_size)])

    last = []

    def gate(*values):
        held = lax.optimization_barrier((values, tuple(last)))[0]
        return held[0] if len(held) == 1 else held

    def mark(*values):
        last[:] = values
        return values[0]

    def partial_sums(block, scale):
        product = dot(block.reshape(-1, fac_width), chol_factor, CONTRACT_LAST)
        if scale is not None:
            product = product * scale
        return product.reshape(block.shape[0], fac_size, chunk_rows, row_block)

    def reduce_over_fac(block, scale, kind):
        terms = partial_sums(gate(block), scale)
        running = None
        for hop in range(fac_size):
            term = terms[:, hop]
            if running is not None:
                term = term + gate(running).astype(jnp.float32)
            if hop < fac_size - 1:
                running = pass_on(mark(term.astype(kind)))
                yield None
        yield mark(term).reshape(-1, half_steps, share, row_block)

    def gather_over_fac(piece):
        pieces = [mark(piece)]
        for _ in range(fac_size - 1):
            pieces.append(pass_on(pieces[-1]))
            yield pieces[:-1]
            pieces[-1] = mark(gate(pieces[-1]))
        yield pieces

    by_share = shocks.reshape(HALVES, half_steps, fac_size, share, fac_width)
    ordered = jnp.stack(
        [
            lax.dynamic_index_in_dim(by_share, (fac_index - 1 - s) % fac_size, axis=2, keepdims=False)
            for s in range(fac_size)
        ],
        axis=1,
    ).reshape(HALVES, fac_size * chunk_rows, fac_width)

    own = mark(ordered[0])
    received = [exchange(own, k) for k in even]
    chain_a = reduce_over_fac(jnp.stack([own, exchange(own, 1)]), None, jnp.float32)
    next(chain_a)

    row_peak = jnp.max(jnp.abs(chol_factor), axis=1).astype(jnp.float32)
    vols, note = gate(factor_vol), None
    bit = 1
    while bit < fac_size:
        note = mark(jnp.concatenate([vols, row_peak]))
        swap = [(i, i ^ bit) for i in range(fac_size)]
        arrived = lax.ppermute(note, "fac", swap)
        next(chain_a)
        arrived = gate(arrived)
        split = arrived.shape[0] - row_block
        lower = (fac_index & bit) == 0
        vols = jnp.where(
            lower,
            jnp.concatenate([vols, arrived[:split]]),
            jnp.concatenate([arrived[:split], vols]),
        )
        row_peak = jnp.maximum(row_peak, arrived[split:])
        bit *= 2
    vol = lax.dynamic_slice(vols, (path_index * row_block,), (row_block,)) / math.sqrt(step_count)
    peak = jnp.clip(row_peak, 1e-30, 1e37) * (6.0 * factor_count / 49152.0)
    shrink = 1.0 / peak
    mark(shrink)

    trade_blocks = trade_loading.reshape(path_size, row_block, trade_count)
    basis_blocks = basis_loading.T.reshape(-1, path_size, row_block).transpose(1, 0, 2)
    local_set = trade_set % sets_here
    member = (local_set[:, None] == jnp.arange(sets_here, dtype=jnp.int32)[None, :]).astype(
        jnp.bfloat16
    )

    def levels_of(increments, carry):
        levels = []
        for step in range(half_steps):
            carry = carry + increments[:, step]
            levels.append((carry * vol).astype(jnp.bfloat16))
        return jnp.stack(levels, axis=1).reshape(-1, chunk_rows, row_block), carry

    def regroup(mine, others):
        arrived = exchange(mark(others), 1)
        yield None
        pairs = mark(jnp.stack([mine, gate(arrived)], axis=1))
        pairs = [pairs[0]] + [exchange(pairs[k // 2], k) for k in even]
        yield None
        yield jnp.concatenate(gate(*pairs), axis=0)

    def started(pieces):
        sums = start_price(gate(*pieces), trade_blocks, basis_blocks, place)
        mark(*sums)
        return sums

    def priced(pieces, sums):
        kept, given, basis = price(
            pieces[-1], trade_blocks, basis_blocks, sums, place, half_steps, path_count
        )
        mark(given)
        return kept, given, basis

    def finish(kept, given, basis, half):
        arrived = exchange(given, 1)
        yield None
        total = mark(kept + gate(arrived))
        rows = total.shape[0] // 2
        top, bottom = total[:rows], total[rows:]
        for n, bit in enumerate(bits):
            more = exchange(top, bit), exchange(bottom, bits[-1 - n])
            yield None
            more = gate(*more)
            if n < len(bits) - 1:
                top, bottom = top + more[0], bottom + more[1]
                mark(top, bottom)
        coef = mark(solve((top, bottom, *more), trade_count, ridge))
        other = exchange(coef, 1)
        so_far = yield None
        yield mark(expose(place, basis, coef, gate(other), member, half, so_far))

    for _ in range(fac_size - 2 - (fac_size.bit_length() - 1)):
        next(chain_a)
    rest = mark(jnp.stack(gate(*received)))
    arrived = exchange(rest, 1)
    chain_b = reduce_over_fac(rest, shrink, jnp.float16)
    next(chain_b)
    own = gate(ordered[1])
    received = [exchange(own, k) for k in even]
    near_sum = next(chain_a)
    chain_c = reduce_over_fac(arrived, shrink, jnp.float16)
    next(chain_c)
    for hop in range(1, fac_size - 1):
        next(chain_b)
        next(chain_c)
    block = mark(jnp.stack([own, *gate(*received)]))
    arrived = exchange(block, 1)
    chain_d = reduce_over_fac(block, shrink, jnp.float16)
    next(chain_d)
    mine = jnp.concatenate([near_sum[:1], next(chain_b) * peak])
    mine, carry = levels_of(mine, 0.0)
    others = jnp.concatenate([near_sum[1:], next(chain_c) * peak])
    others, other_carry = levels_of(others, 0.0)
    first = regroup(mine, others)
    next(first)
    next(first)
    chain_e = reduce_over_fac(arrived, shrink, jnp.float16)
    next(chain_e)
    next(chain_d)
    next(chain_e)
    ring_first = gather_over_fac(next(first))
    next(ring_first)
    for hop in range(2, fac_size - 1):
        next(chain_d)
        next(chain_e)
    mine, others = next(chain_d) * peak, next(chain_e) * peak
    others, _ = levels_of(others, other_carry)
    mine, _ = levels_of(mine, carry)
    second = regroup(mine, others)
    next(second)
    next(second)
    next(ring_first)
    ring_second = gather_over_fac(next(second))
    next(ring_second)
    for hop in range(2, fac_size - 1):
        pieces = next(ring_first)
        next(ring_second)
    head = started(pieces)
    first = finish(*priced(next(ring_first), head), 0)
    next(first)
    next(first)
    pieces = next(ring_second)
    for _ in bits[1:]:
        next(first)
    head = started(pieces)
    next(first)
    second = finish(*priced(next(ring_second), head), 1)
    for _ in range(len(bits) + 1):
        next(second)
    result = next(first)
    next(second)
    return second.send(result)


def solution(mesh):
    in_specs = (P(None, "path", "fac"), P("path", "fac"), P("fac"), P(None, "fac"), P(), P("fac"))
    out_specs = P(None, "path", "fac")
    return jax.shard_map(
        on_device, mesh=mesh, in_specs=in_specs, out_specs=out_specs, check_vma=False
    )
```

```python
import functools
import math

import jax
import jax.numpy as jnp
from jax import lax
from jax.experimental import pallas as pl
from jax.experimental.pallas import tpu as pltpu
from jax.sharding import PartitionSpec as P

NSETS = 4096
HALVES = 2
VMEM_LIMIT = 24 * 2**20
HIGHEST = lax.Precision.HIGHEST
CONTRACT_LAST = (((1,), (1,)), ((), ()))
CONTRACT_FIRST = (((0,), (0,)), ((), ()))


def dot(a, b, dims, precision=None):
    return lax.dot_general(a, b, dims, precision=precision, preferred_element_type=jnp.float32)


def accumulate(place, pieces, trade, basis_load):
    fac_parts = len(pieces)
    blocks, rows, _ = pieces[0].shape
    drivers = jnp.zeros((fac_parts * rows, trade.shape[2]), jnp.float32)
    projected = jnp.zeros((fac_parts * rows, basis_load.shape[1]), jnp.float32)
    for n in range(blocks):
        levels = jnp.concatenate([piece[n] for piece in pieces], axis=0)
        factors = place[2 + n]
        drivers += jnp.dot(levels, trade[factors], preferred_element_type=jnp.float32)
        projected += dot(levels, basis_load[factors], CONTRACT_LAST)
    return drivers, projected


def start_price_kernel(place, *refs):
    trade, basis_load, drivers, projected = refs[-4:]
    drivers[...], projected[...] = accumulate(place, refs[:-4], trade, basis_load)


def price_kernel(place, piece, trade, basis_load, drivers, projected, kept, given, ordered):
    rows = piece.shape[1]
    fac_size = drivers.shape[0] // rows + 1
    last_drivers, last_projected = accumulate(place, [piece], trade, basis_load)
    drivers = jnp.concatenate([drivers[...], last_drivers], axis=0)
    values = jnp.maximum(drivers, 0.0) + jnp.log1p(jnp.exp(-jnp.abs(drivers))) - 1.0
    basis = jnp.tanh(jnp.concatenate([projected[...], last_projected], axis=0))
    steps, paths, basis_count = ordered.shape
    share = paths // fac_size
    fac_index, core = place[0], place[1]
    sums = []
    for step in range(steps):
        spans = [
            slice((hop * steps + step) * share, (hop * steps + step + 1) * share)
            for hop in range(fac_size)
        ]
        for hop in range(fac_size):
            source = lax.rem(fac_index - hop + fac_size, fac_size)
            at = pl.multiple_of(source * share, share)
            ordered[step, pl.ds(at, share), :] = basis[spans[hop]]
        step_basis = jnp.concatenate([basis[s] for s in spans], axis=0)
        step_values = jnp.concatenate([values[s] for s in spans], axis=0)
        joint = jnp.concatenate([step_values, step_basis, step_basis], axis=1)
        sums.append(dot(step_basis, joint, CONTRACT_FIRST, HIGHEST))
    kept[...] = jnp.where(core == 0, sums[0], sums[1])
    given[...] = jnp.where(core == 0, sums[1], sums[0])


def start_price(pieces, trade_blocks, basis_blocks, place):
    blocks, rows, width = pieces[0].shape
    rows = len(pieces) * rows
    trades, basis_count = trade_blocks.shape[2], basis_blocks.shape[1]
    vmem = pl.BlockSpec(memory_space=pltpu.VMEM)
    return pl.pallas_call(
        start_price_kernel,
        in_specs=[pl.BlockSpec(memory_space=pltpu.SMEM)] + [vmem] * (len(pieces) + 2),
        out_specs=[vmem] * 2,
        out_shape=[
            jax.ShapeDtypeStruct((rows, trades), jnp.float32),
            jax.ShapeDtypeStruct((rows, basis_count), jnp.float32),
        ],
        compiler_params=pltpu.CompilerParams(vmem_limit_bytes=VMEM_LIMIT),
        cost_estimate=pl.CostEstimate(
            flops=2 * rows * blocks * width * (trades + basis_count),
            bytes_accessed=2 * blocks * width * (trades + rows),
            transcendentals=0,
        ),
        name="start_price",
    )(place, *pieces, trade_blocks, basis_blocks)


def price(piece, trade_blocks, basis_blocks, started, place, steps, paths):
    blocks, rows, width = piece.shape
    trades, basis_count = trade_blocks.shape[2], basis_blocks.shape[1]
    sums = jax.ShapeDtypeStruct((basis_count, trades + 2 * basis_count), jnp.float32)
    vmem = pl.BlockSpec(memory_space=pltpu.VMEM)
    return pl.pallas_call(
        price_kernel,
        in_specs=[pl.BlockSpec(memory_space=pltpu.SMEM)] + [vmem] * 5,
        out_specs=[vmem] * 3,
        out_shape=[sums, sums, jax.ShapeDtypeStruct((steps, paths, basis_count), jnp.float32)],
        compiler_params=pltpu.CompilerParams(vmem_limit_bytes=VMEM_LIMIT),
        cost_estimate=pl.CostEstimate(
            flops=2 * rows * blocks * width * (trades + basis_count),
            bytes_accessed=2 * blocks * width * (trades + rows),
            transcendentals=2 * steps * paths * trades,
        ),
        name="price",
    )(place, piece, trade_blocks, basis_blocks, *started)


def solve_kernel(ridge, first_top, first_bottom, second_top, second_bottom, coef):
    count, trades = coef.shape
    sums = jnp.concatenate(
        [first_top[...] + second_top[...], first_bottom[...] + second_bottom[...]], axis=0
    )
    row = lax.broadcasted_iota(jnp.int32, (count, 2 * count), 0)
    lane = lax.broadcasted_iota(jnp.int32, (count, 2 * count), 1)
    work = jnp.where(lane < count, sums[:, trades:], 0.0)
    work = work + jnp.where(lane == row, ridge, 0.0) + jnp.where(lane == row + count, 1.0, 0.0)
    for j in range(0, count, 2):
        left = jnp.broadcast_to(work[:, j : j + 1], work.shape)
        right = jnp.broadcast_to(work[:, j + 1 : j + 2], work.shape)
        upper, lower = work[j : j + 1, :], work[j + 1 : j + 2, :]
        a, b = left[j : j + 1, :], right[j : j + 1, :]
        c, d = left[j + 1 : j + 2, :], right[j + 1 : j + 2, :]
        scale = 1.0 / (a * d - b * c)
        new_upper = (d * upper - b * lower) * scale
        new_lower = (a * lower - c * upper) * scale
        work = work - left * new_upper - right * new_lower
        work = jnp.where(row == j, new_upper, jnp.where(row == j + 1, new_lower, work))
    coef[...] = jnp.dot(
        work[:, count:], sums[:, :trades], precision=HIGHEST, preferred_element_type=jnp.float32
    )


def solve(parts, trades, ridge):
    count = 2 * parts[0].shape[0]
    return pl.pallas_call(
        functools.partial(solve_kernel, ridge),
        out_shape=jax.ShapeDtypeStruct((count, trades), jnp.float32),
        compiler_params=pltpu.CompilerParams(vmem_limit_bytes=VMEM_LIMIT),
        cost_estimate=pl.CostEstimate(
            flops=2 * count**3 + 12 * count * count * trades,
            bytes_accessed=4 * count * trades * 3,
            transcendentals=0,
        ),
        name="solve",
    )(*parts)


def expose_kernel(place, basis, mine, other, member, *refs):
    out = refs[-1]
    core = place[1]
    steps, paths, sets = out.shape
    by_trade = jnp.concatenate(
        [
            jnp.dot(
                basis[step],
                jnp.where(core == step, mine[...], other[...]),
                precision=HIGHEST,
                preferred_element_type=jnp.float32,
            )
            for step in range(steps)
        ],
        axis=0,
    )
    terms = []
    for _ in range(3):
        term = by_trade.astype(jnp.bfloat16)
        by_trade = by_trade - term.astype(jnp.float32)
        terms.append(term)
    spread = [jnp.dot(t, member[...], preferred_element_type=jnp.float32) for t in terms]
    total = jnp.maximum(spread[0] + (spread[1] + spread[2]), 0.0)
    for step in range(steps):
        out[step] = total[step * paths : (step + 1) * paths]


def expose(place, basis, mine, other, member, half, so_far):
    steps, paths, _ = basis.shape
    trades, sets = member.shape
    vmem = pl.BlockSpec(memory_space=pltpu.VMEM)
    block = pl.BlockSpec((steps, paths, sets), lambda i: (half, 0, 0))
    earlier = [] if so_far is None else [so_far]
    return pl.pallas_call(
        expose_kernel,
        grid=(1,),
        in_specs=[pl.BlockSpec(memory_space=pltpu.SMEM)]
        + [vmem] * 4
        + [pl.BlockSpec(memory_space=pl.ANY)] * len(earlier),
        out_specs=block,
        out_shape=jax.ShapeDtypeStruct((HALVES * steps, paths, sets), jnp.float32),
        input_output_aliases={5: 0} if earlier else {},
        compiler_params=pltpu.CompilerParams(vmem_limit_bytes=VMEM_LIMIT),
        cost_estimate=pl.CostEstimate(
            flops=6 * steps * paths * trades * sets,
            bytes_accessed=4 * steps * paths * sets * 2,
            transcendentals=0,
        ),
        name="expose",
    )(place, basis, mine, other, member, *earlier)


def on_device(shocks, chol_factor, factor_vol, trade_loading, basis_loading, trade_set):
    step_count, path_count, fac_width = shocks.shape
    row_block = chol_factor.shape[0]
    factor_count, trade_count = trade_loading.shape
    path_size, fac_size = lax.axis_size("path"), lax.axis_size("fac")
    path_index, fac_index = lax.axis_index("path"), lax.axis_index("fac")
    share = path_count // fac_size
    half_steps = step_count // HALVES
    chunk_rows = half_steps * share
    sets_here = NSETS // fac_size
    ridge = 0.01 * path_count * path_size
    even = list(range(2, path_size, 2))
    bits = [2**n for n in range(1, path_size.bit_length() - 1)]
    core = path_index & 1
    place = jnp.concatenate(
        [
            jnp.stack([fac_index, path_index & 1]),
            path_index ^ jnp.arange(path_size, dtype=jnp.int32),
        ]
    ).astype(jnp.int32)

    def exchange(x, k, k_odd=None):
        far = [k, k if k_odd is None else k_odd]
        return lax.ppermute(x, "path", [(i, i ^ far[i & 1]) for i in range(path_size)])

    def pass_on(x, hops=1):
        return lax.ppermute(x, "fac", [(i, (i + hops) % fac_size) for i in range(fac_size)])

    last = []

    def gate(*values):
        held = lax.optimization_barrier((values, tuple(last)))[0]
        return held[0] if len(held) == 1 else held

    def mark(*values):
        last[:] = values
        return values[0]

    def partial_sums(block, scale):
        product = dot(block.reshape(-1, fac_width), chol_factor, CONTRACT_LAST)
        if scale is not None:
            product = product * scale
        return product.reshape(block.shape[0], fac_size, chunk_rows, row_block)

    def reduce_over_fac(block, scale, kind):
        return ring_sum([partial_sums(gate(block), scale)], kind)

    def ring_sum(terms, kind, scale=None):
        running = None
        for hop in range(fac_size):
            term = jnp.concatenate([t[:, hop] for t in terms])
            if scale is not None:
                term = term * scale
            if running is not None:
                term = term + gate(running).astype(jnp.float32)
            if hop < fac_size - 1:
                running = pass_on(mark(term.astype(kind)))
                yield None
        yield mark(term).reshape(-1, half_steps, share, row_block)

    def gather_over_fac(piece):
        pieces = [mark(piece)]
        for _ in range(fac_size - 1):
            pieces.append(pass_on(pieces[-1]))
            yield pieces[:-1]
            pieces[-1] = mark(gate(pieces[-1]))
        yield pieces

    by_share = shocks.reshape(HALVES, half_steps, fac_size, share, fac_width)
    ordered = jnp.stack(
        [
            lax.dynamic_index_in_dim(by_share, (fac_index - 1 - s) % fac_size, axis=2, keepdims=False)
            for s in range(fac_size)
        ],
        axis=1,
    ).reshape(HALVES, fac_size * chunk_rows, fac_width)

    own = mark(ordered[0])
    two_bits = len(bits) == 2
    received = [exchange(own, k) for k in (bits if two_bits else even)]
    siblings = exchange(ordered, 1)

    row_peak = jnp.max(jnp.abs(chol_factor), axis=1).astype(jnp.float32)
    vols, note = gate(factor_vol), None
    bit = 1
    while bit < fac_size:
        note = mark(jnp.concatenate([vols, row_peak]))
        swap = [(i, i ^ bit) for i in range(fac_size)]
        arrived = lax.ppermute(note, "fac", swap)
        if 2 * bit >= fac_size:
            near_terms = mark(partial_sums(gate(jnp.concatenate([ordered, siblings])), None))
        arrived = gate(arrived)
        split = arrived.shape[0] - row_block
        lower = (fac_index & bit) == 0
        vols = jnp.where(
            lower,
            jnp.concatenate([vols, arrived[:split]]),
            jnp.concatenate([arrived[:split], vols]),
        )
        row_peak = jnp.maximum(row_peak, arrived[split:])
        bit *= 2
    vol = lax.dynamic_slice(vols, (path_index * row_block,), (row_block,)) / math.sqrt(step_count)
    peak = jnp.clip(row_peak, 1e-30, 1e37) * (6.0 * factor_count / 49152.0)
    shrink = 1.0 / peak
    mark(shrink)

    trade_blocks = trade_loading.reshape(path_size, row_block, trade_count)
    basis_blocks = basis_loading.T.reshape(-1, path_size, row_block).transpose(1, 0, 2)
    local_set = trade_set % sets_here
    member = (local_set[:, None] == jnp.arange(sets_here, dtype=jnp.int32)[None, :]).astype(
        jnp.bfloat16
    )

    def levels_of(increments, carry):
        levels = []
        for step in range(half_steps):
            carry = carry + increments[:, step]
            levels.append((carry * vol).astype(jnp.bfloat16))
        return jnp.stack(levels, axis=1).reshape(-1, chunk_rows, row_block), carry

    def regroup(mine, others):
        arrived = exchange(mark(others), 1)
        yield None
        pairs = mark(jnp.stack([mine, gate(arrived)], axis=1))
        pairs = [pairs[0]] + [exchange(pairs[k // 2], k) for k in even]
        yield None
        yield jnp.concatenate(gate(*pairs), axis=0)

    def started(pieces):
        sums = start_price(gate(*pieces), trade_blocks, basis_blocks, place)
        mark(*sums)
        return sums

    def priced(pieces, sums):
        kept, given, basis = price(
            pieces[-1], trade_blocks, basis_blocks, sums, place, half_steps, path_count
        )
        mark(given)
        return kept, given, basis

    def finish(kept, given, basis, half):
        arrived = exchange(given, 1)
        yield None
        total = mark(kept + gate(arrived))
        rows = total.shape[0] // 2
        top, bottom = total[:rows], total[rows:]
        for n, bit in enumerate(bits):
            more = exchange(top, bit), exchange(bottom, bits[-1 - n])
            yield None
            more = gate(*more)
            if n < len(bits) - 1:
                top, bottom = top + more[0], bottom + more[1]
                mark(top, bottom)
        coef = mark(solve((top, bottom, *more), trade_count, ridge))
        other = exchange(coef, 1)
        so_far = yield None
        yield mark(expose(place, basis, coef, gate(other), member, half, so_far))

    chain_a = ring_sum([near_terms], jnp.float16, shrink)
    next(chain_a)
    for _ in range(fac_size - 4):
        next(chain_a)
    if two_bits:
        received = gate(*received)
        third = exchange(mark(jnp.where(core == 0, *received)), bits[1], bits[0])
        rest = mark(jnp.stack(received))
        arrived_rest = exchange(rest, 1)
        own_terms = [mark(partial_sums(rest, None))]
        next(chain_a)
        swapped_terms = [mark(partial_sums(gate(arrived_rest), None))]
        rest = mark(gate(third)[None])
        third = exchange(rest, 1)
        own_terms.append(partial_sums(rest, None))
        chain_b = ring_sum(own_terms, jnp.float16, shrink)
        next(chain_b)
    else:
        next(chain_a)
        rest = mark(jnp.stack(gate(*received)))
        third = exchange(rest, 1)
        swapped_terms = []
        chain_b = ring_sum([partial_sums(rest, None)], jnp.float16, shrink)
        next(chain_b)
    own = gate(ordered[1])
    received = [exchange(own, k) for k in (bits if two_bits else even)]
    next(chain_a)
    swapped_terms.append(partial_sums(gate(third), None))
    chain_c = ring_sum(swapped_terms, jnp.float16, shrink)
    next(chain_c)
    next(chain_b)
    near_sum = next(chain_a) * peak
    if two_bits:
        received = list(gate(*received))
        third_late = exchange(mark(jnp.where(core == 0, *received)), bits[1], bits[0])
    next(chain_c)
    for hop in range(2, fac_size - 1):
        next(chain_b)
        next(chain_c)
    if two_bits:
        received = [*received, gate(third_late)]
        block = mark(jnp.stack(received))
    else:
        block = mark(jnp.stack(gate(*received)))
    arrived = exchange(block, 1)
    chain_d = reduce_over_fac(block, shrink, jnp.float16)
    next(chain_d)
    chain_e = reduce_over_fac(arrived, shrink, jnp.float16)
    next(chain_e)
    next(chain_d)
    mine = jnp.concatenate([near_sum[0:1], next(chain_b) * peak])
    mine, carry = levels_of(mine, 0.0)
    others = jnp.concatenate([near_sum[2:3], next(chain_c) * peak])
    others, other_carry = levels_of(others, 0.0)
    first = regroup(mine, others)
    next(first)
    next(first)
    next(chain_e)
    for hop in range(2, fac_size - 1):
        next(chain_d)
        next(chain_e)
    ring_first = gather_over_fac(next(first))
    next(ring_first)
    mine = jnp.concatenate([near_sum[1:2], next(chain_d) * peak])
    others = jnp.concatenate([near_sum[3:4], next(chain_e) * peak])
    others, _ = levels_of(others, other_carry)
    mine, _ = levels_of(mine, carry)
    second = regroup(mine, others)
    next(second)
    next(second)
    next(ring_first)
    ring_second = gather_over_fac(next(second))
    next(ring_second)
    for hop in range(2, fac_size - 1):
        pieces = next(ring_first)
        next(ring_second)
    head = started(pieces)
    first = finish(*priced(next(ring_first), head), 0)
    next(first)
    next(first)
    pieces = next(ring_second)
    for _ in bits[1:]:
        next(first)
    head = started(pieces)
    next(first)
    second = finish(*priced(next(ring_second), head), 1)
    for _ in range(len(bits) + 1):
        next(second)
    result = next(first)
    next(second)
    return second.send(result)


def solution(mesh):
    in_specs = (P(None, "path", "fac"), P("path", "fac"), P("fac"), P(None, "fac"), P(), P("fac"))
    out_specs = P(None, "path", "fac")
    return jax.shard_map(
        on_device, mesh=mesh, in_specs=in_specs, out_specs=out_specs, check_vma=False
    )
```

```python
import functools
import math

import jax
import jax.numpy as jnp
from jax import lax
from jax.experimental import pallas as pl
from jax.experimental.pallas import tpu as pltpu
from jax.sharding import PartitionSpec as P

NSETS = 4096
HALVES = 2
VMEM_LIMIT = 24 * 2**20
HIGHEST = lax.Precision.HIGHEST
CONTRACT_LAST = (((1,), (1,)), ((), ()))
CONTRACT_FIRST = (((0,), (0,)), ((), ()))


def dot(a, b, dims, precision=None):
    return lax.dot_general(a, b, dims, precision=precision, preferred_element_type=jnp.float32)


def accumulate(place, pieces, trade, basis_load):
    fac_parts = len(pieces)
    blocks, rows, _ = pieces[0].shape
    drivers = jnp.zeros((fac_parts * rows, trade.shape[2]), jnp.float32)
    projected = jnp.zeros((fac_parts * rows, basis_load.shape[1]), jnp.float32)
    for n in range(blocks):
        levels = jnp.concatenate([piece[n] for piece in pieces], axis=0)
        factors = place[2 + n]
        drivers += jnp.dot(levels, trade[factors], preferred_element_type=jnp.float32)
        projected += dot(levels, basis_load[factors], CONTRACT_LAST)
    return drivers, projected


def start_price_kernel(place, *refs):
    trade, basis_load, drivers, projected = refs[-4:]
    drivers[...], projected[...] = accumulate(place, refs[:-4], trade, basis_load)


def price_kernel(place, piece, trade, basis_load, drivers, projected, kept, given, ordered):
    rows = piece.shape[1]
    fac_size = drivers.shape[0] // rows + 1
    last_drivers, last_projected = accumulate(place, [piece], trade, basis_load)
    drivers = jnp.concatenate([drivers[...], last_drivers], axis=0)
    values = jnp.maximum(drivers, 0.0) + jnp.log1p(jnp.exp(-jnp.abs(drivers))) - 1.0
    basis = jnp.tanh(jnp.concatenate([projected[...], last_projected], axis=0))
    steps, paths, basis_count = ordered.shape
    share = paths // fac_size
    fac_index, core = place[0], place[1]
    sums = []
    for step in range(steps):
        spans = [
            slice((hop * steps + step) * share, (hop * steps + step + 1) * share)
            for hop in range(fac_size)
        ]
        for hop in range(fac_size):
            source = lax.rem(fac_index - hop + fac_size, fac_size)
            at = pl.multiple_of(source * share, share)
            ordered[step, pl.ds(at, share), :] = basis[spans[hop]]
        step_basis = jnp.concatenate([basis[s] for s in spans], axis=0)
        step_values = jnp.concatenate([values[s] for s in spans], axis=0)
        joint = jnp.concatenate([step_values, step_basis, step_basis], axis=1)
        sums.append(dot(step_basis, joint, CONTRACT_FIRST, HIGHEST))
    kept[...] = jnp.where(core == 0, sums[0], sums[1])
    given[...] = jnp.where(core == 0, sums[1], sums[0])


def start_price(pieces, trade_blocks, basis_blocks, place):
    blocks, rows, width = pieces[0].shape
    rows = len(pieces) * rows
    trades, basis_count = trade_blocks.shape[2], basis_blocks.shape[1]
    vmem = pl.BlockSpec(memory_space=pltpu.VMEM)
    return pl.pallas_call(
        start_price_kernel,
        in_specs=[pl.BlockSpec(memory_space=pltpu.SMEM)] + [vmem] * (len(pieces) + 2),
        out_specs=[vmem] * 2,
        out_shape=[
            jax.ShapeDtypeStruct((rows, trades), jnp.float32),
            jax.ShapeDtypeStruct((rows, basis_count), jnp.float32),
        ],
        compiler_params=pltpu.CompilerParams(vmem_limit_bytes=VMEM_LIMIT),
        cost_estimate=pl.CostEstimate(
            flops=2 * rows * blocks * width * (trades + basis_count),
            bytes_accessed=2 * blocks * width * (trades + rows),
            transcendentals=0,
        ),
        name="start_price",
    )(place, *pieces, trade_blocks, basis_blocks)


def price(piece, trade_blocks, basis_blocks, started, place, steps, paths):
    blocks, rows, width = piece.shape
    trades, basis_count = trade_blocks.shape[2], basis_blocks.shape[1]
    sums = jax.ShapeDtypeStruct((basis_count, trades + 2 * basis_count), jnp.float32)
    vmem = pl.BlockSpec(memory_space=pltpu.VMEM)
    return pl.pallas_call(
        price_kernel,
        in_specs=[pl.BlockSpec(memory_space=pltpu.SMEM)] + [vmem] * 5,
        out_specs=[vmem] * 3,
        out_shape=[sums, sums, jax.ShapeDtypeStruct((steps, paths, basis_count), jnp.float32)],
        compiler_params=pltpu.CompilerParams(vmem_limit_bytes=VMEM_LIMIT),
        cost_estimate=pl.CostEstimate(
            flops=2 * rows * blocks * width * (trades + basis_count),
            bytes_accessed=2 * blocks * width * (trades + rows),
            transcendentals=2 * steps * paths * trades,
        ),
        name="price",
    )(place, piece, trade_blocks, basis_blocks, *started)


def solve_kernel(ridge, first_top, first_bottom, second_top, second_bottom, coef):
    count, trades = coef.shape
    sums = jnp.concatenate(
        [first_top[...] + second_top[...], first_bottom[...] + second_bottom[...]], axis=0
    )
    row = lax.broadcasted_iota(jnp.int32, (count, 2 * count), 0)
    lane = lax.broadcasted_iota(jnp.int32, (count, 2 * count), 1)
    work = jnp.where(lane < count, sums[:, trades:], 0.0)
    work = work + jnp.where(lane == row, ridge, 0.0) + jnp.where(lane == row + count, 1.0, 0.0)
    for j in range(0, count, 2):
        left = jnp.broadcast_to(work[:, j : j + 1], work.shape)
        right = jnp.broadcast_to(work[:, j + 1 : j + 2], work.shape)
        upper, lower = work[j : j + 1, :], work[j + 1 : j + 2, :]
        a, b = left[j : j + 1, :], right[j : j + 1, :]
        c, d = left[j + 1 : j + 2, :], right[j + 1 : j + 2, :]
        scale = 1.0 / (a * d - b * c)
        new_upper = (d * upper - b * lower) * scale
        new_lower = (a * lower - c * upper) * scale
        work = work - left * new_upper - right * new_lower
        work = jnp.where(row == j, new_upper, jnp.where(row == j + 1, new_lower, work))
    coef[...] = jnp.dot(
        work[:, count:], sums[:, :trades], precision=HIGHEST, preferred_element_type=jnp.float32
    )


def solve(parts, trades, ridge):
    count = 2 * parts[0].shape[0]
    return pl.pallas_call(
        functools.partial(solve_kernel, ridge),
        out_shape=jax.ShapeDtypeStruct((count, trades), jnp.float32),
        compiler_params=pltpu.CompilerParams(vmem_limit_bytes=VMEM_LIMIT),
        cost_estimate=pl.CostEstimate(
            flops=2 * count**3 + 12 * count * count * trades,
            bytes_accessed=4 * count * trades * 3,
            transcendentals=0,
        ),
        name="solve",
    )(*parts)


def expose_kernel(place, basis, mine, other, member, *refs):
    out = refs[-1]
    core = place[1]
    steps, paths, sets = out.shape
    by_trade = jnp.concatenate(
        [
            jnp.dot(
                basis[step],
                jnp.where(core == step, mine[...], other[...]),
                precision=HIGHEST,
                preferred_element_type=jnp.float32,
            )
            for step in range(steps)
        ],
        axis=0,
    )
    terms = []
    for _ in range(3):
        term = by_trade.astype(jnp.bfloat16)
        by_trade = by_trade - term.astype(jnp.float32)
        terms.append(term)
    spread = [jnp.dot(t, member[...], preferred_element_type=jnp.float32) for t in terms]
    total = jnp.maximum(spread[0] + (spread[1] + spread[2]), 0.0)
    for step in range(steps):
        out[step] = total[step * paths : (step + 1) * paths]


def expose(place, basis, mine, other, member, half, so_far):
    steps, paths, _ = basis.shape
    trades, sets = member.shape
    vmem = pl.BlockSpec(memory_space=pltpu.VMEM)
    block = pl.BlockSpec((steps, paths, sets), lambda i: (half, 0, 0))
    earlier = [] if so_far is None else [so_far]
    return pl.pallas_call(
        expose_kernel,
        grid=(1,),
        in_specs=[pl.BlockSpec(memory_space=pltpu.SMEM)]
        + [vmem] * 4
        + [pl.BlockSpec(memory_space=pl.ANY)] * len(earlier),
        out_specs=block,
        out_shape=jax.ShapeDtypeStruct((HALVES * steps, paths, sets), jnp.float32),
        input_output_aliases={5: 0} if earlier else {},
        compiler_params=pltpu.CompilerParams(vmem_limit_bytes=VMEM_LIMIT),
        cost_estimate=pl.CostEstimate(
            flops=6 * steps * paths * trades * sets,
            bytes_accessed=4 * steps * paths * sets * 2,
            transcendentals=0,
        ),
        name="expose",
    )(place, basis, mine, other, member, *earlier)


def on_device(shocks, chol_factor, factor_vol, trade_loading, basis_loading, trade_set):
    step_count, path_count, fac_width = shocks.shape
    row_block = chol_factor.shape[0]
    factor_count, trade_count = trade_loading.shape
    path_size, fac_size = lax.axis_size("path"), lax.axis_size("fac")
    path_index, fac_index = lax.axis_index("path"), lax.axis_index("fac")
    share = path_count // fac_size
    half_steps = step_count // HALVES
    chunk_rows = half_steps * share
    sets_here = NSETS // fac_size
    ridge = 0.01 * path_count * path_size
    even = list(range(2, path_size, 2))
    bits = [2**n for n in range(1, path_size.bit_length() - 1)]
    core = path_index & 1
    place = jnp.concatenate(
        [
            jnp.stack([fac_index, path_index & 1]),
            path_index ^ jnp.arange(path_size, dtype=jnp.int32),
        ]
    ).astype(jnp.int32)

    def exchange(x, k, k_odd=None):
        far = [k, k if k_odd is None else k_odd]
        return lax.ppermute(x, "path", [(i, i ^ far[i & 1]) for i in range(path_size)])

    def pass_on(x, hops=1):
        return lax.ppermute(x, "fac", [(i, (i + hops) % fac_size) for i in range(fac_size)])

    last = []

    def gate(*values):
        held = lax.optimization_barrier((values, tuple(last)))[0]
        return held[0] if len(held) == 1 else held

    def mark(*values):
        last[:] = values
        return values[0]

    def partial_sums(block, scale):
        product = dot(block.reshape(-1, fac_width), chol_factor, CONTRACT_LAST)
        if scale is not None:
            product = product * scale
        return product.reshape(block.shape[0], fac_size, chunk_rows, row_block)

    def reduce_over_fac(block, scale, kind):
        return ring_sum([partial_sums(gate(block), scale)], kind)

    def ring_sum(terms, kind, scale=None):
        running = None
        for hop in range(fac_size):
            term = jnp.concatenate([t[:, hop] for t in terms])
            if scale is not None:
                term = term * scale
            if running is not None:
                term = term + gate(running).astype(jnp.float32)
            if hop < fac_size - 1:
                running = pass_on(mark(term.astype(kind)))
                yield None
        yield mark(term).reshape(-1, half_steps, share, row_block)

    def gather_over_fac(piece):
        pieces = [mark(piece)]
        for _ in range(fac_size - 1):
            pieces.append(pass_on(pieces[-1]))
            yield pieces[:-1]
            pieces[-1] = mark(gate(pieces[-1]))
        yield pieces

    by_share = shocks.reshape(HALVES, half_steps, fac_size, share, fac_width)
    ordered = jnp.stack(
        [
            lax.dynamic_index_in_dim(by_share, (fac_index - 1 - s) % fac_size, axis=2, keepdims=False)
            for s in range(fac_size)
        ],
        axis=1,
    ).reshape(HALVES, fac_size * chunk_rows, fac_width)

    own = mark(ordered[0])
    two_bits = len(bits) == 2
    received = [exchange(own, k) for k in (bits if two_bits else even)]
    siblings = exchange(ordered, 1)

    row_peak = jnp.max(jnp.abs(chol_factor), axis=1).astype(jnp.float32)
    siblings = mark(gate(siblings))
    vols, row_peak = gate(factor_vol, row_peak)
    bit = 1
    while bit < fac_size:
        note = mark(jnp.concatenate([vols, row_peak]))
        swap = [(i, i ^ bit) for i in range(fac_size)]
        arrived = lax.ppermute(note, "fac", swap)
        if 2 * bit >= fac_size:
            near_terms = mark(partial_sums(gate(jnp.concatenate([ordered, siblings])), None))
        arrived = gate(arrived)
        split = arrived.shape[0] - row_block
        lower = (fac_index & bit) == 0
        vols = jnp.where(
            lower,
            jnp.concatenate([vols, arrived[:split]]),
            jnp.concatenate([arrived[:split], vols]),
        )
        row_peak = jnp.maximum(row_peak, arrived[split:])
        bit *= 2
    vol = lax.dynamic_slice(vols, (path_index * row_block,), (row_block,)) / math.sqrt(step_count)
    peak = jnp.clip(row_peak, 1e-30, 1e37) * (6.0 * factor_count / 49152.0)
    shrink = 1.0 / peak
    mark(shrink)

    trade_blocks = trade_loading.reshape(path_size, row_block, trade_count)
    basis_blocks = basis_loading.T.reshape(-1, path_size, row_block).transpose(1, 0, 2)
    local_set = trade_set % sets_here
    member = (local_set[:, None] == jnp.arange(sets_here, dtype=jnp.int32)[None, :]).astype(
        jnp.bfloat16
    )

    def levels_of(increments, carry):
        levels = []
        for step in range(half_steps):
            carry = carry + increments[:, step]
            levels.append((carry * vol).astype(jnp.bfloat16))
        return jnp.stack(levels, axis=1).reshape(-1, chunk_rows, row_block), carry

    def regroup(mine, others):
        arrived = exchange(mark(others), 1)
        yield None
        pairs = mark(jnp.stack([mine, gate(arrived)], axis=1))
        pairs = [pairs[0]] + [exchange(pairs[k // 2], k) for k in even]
        yield None
        yield jnp.concatenate(gate(*pairs), axis=0)

    def started(pieces):
        sums = start_price(gate(*pieces), trade_blocks, basis_blocks, place)
        mark(*sums)
        return sums

    def priced(pieces, sums):
        kept, given, basis = price(
            pieces[-1], trade_blocks, basis_blocks, sums, place, half_steps, path_count
        )
        mark(given)
        return kept, given, basis

    def finish(kept, given, basis, half):
        arrived = exchange(given, 1)
        yield None
        total = mark(kept + gate(arrived))
        rows = total.shape[0] // 2
        top, bottom = total[:rows], total[rows:]
        for n, bit in enumerate(bits):
            more = exchange(top, bit), exchange(bottom, bits[-1 - n])
            yield None
            more = gate(*more)
            if n < len(bits) - 1:
                top, bottom = top + more[0], bottom + more[1]
                mark(top, bottom)
        coef = mark(solve((top, bottom, *more), trade_count, ridge))
        other = exchange(coef, 1)
        so_far = yield None
        yield mark(expose(place, basis, coef, gate(other), member, half, so_far))

    chain_a = ring_sum([near_terms], jnp.float16, shrink)
    next(chain_a)
    for _ in range(fac_size - 4):
        next(chain_a)
    if two_bits:
        received = gate(*received)
        third = exchange(mark(jnp.where(core == 0, *received)), bits[1], bits[0])
        rest = mark(jnp.stack(received))
        arrived_rest = exchange(rest, 1)
        own_terms = [mark(partial_sums(rest, None))]
        next(chain_a)
        swapped_terms = [mark(partial_sums(gate(arrived_rest), None))]
        rest = mark(gate(third)[None])
        third = exchange(rest, 1)
        own_terms.append(partial_sums(rest, None))
        chain_b = ring_sum(own_terms, jnp.float16, shrink)
        next(chain_b)
    else:
        next(chain_a)
        rest = mark(jnp.stack(gate(*received)))
        third = exchange(rest, 1)
        swapped_terms = []
        chain_b = ring_sum([partial_sums(rest, None)], jnp.float16, shrink)
        next(chain_b)
    own = gate(ordered[1])
    received = [exchange(own, k) for k in (bits if two_bits else even)]
    next(chain_a)
    swapped_terms.append(partial_sums(gate(third), None))
    chain_c = ring_sum(swapped_terms, jnp.float16, shrink)
    next(chain_c)
    next(chain_b)
    near_sum = next(chain_a) * peak
    if two_bits:
        received = list(gate(*received))
        third_late = exchange(mark(jnp.where(core == 0, *received)), bits[1], bits[0])
    next(chain_c)
    for hop in range(2, fac_size - 1):
        next(chain_b)
        next(chain_c)
    if two_bits:
        received = [*received, gate(third_late)]
        block = mark(jnp.stack(received))
    else:
        block = mark(jnp.stack(gate(*received)))
    arrived = exchange(block, 1)
    chain_d = reduce_over_fac(block, shrink, jnp.float16)
    next(chain_d)
    chain_e = reduce_over_fac(arrived, shrink, jnp.float16)
    next(chain_e)
    next(chain_d)
    mine = jnp.concatenate([near_sum[0:1], next(chain_b) * peak])
    mine, carry = levels_of(mine, 0.0)
    others = jnp.concatenate([near_sum[2:3], next(chain_c) * peak])
    others, other_carry = levels_of(others, 0.0)
    first = regroup(mine, others)
    next(first)
    next(first)
    next(chain_e)
    for hop in range(2, fac_size - 1):
        next(chain_d)
        next(chain_e)
    ring_first = gather_over_fac(next(first))
    next(ring_first)
    mine = jnp.concatenate([near_sum[1:2], next(chain_d) * peak])
    others = jnp.concatenate([near_sum[3:4], next(chain_e) * peak])
    others, _ = levels_of(others, other_carry)
    mine, _ = levels_of(mine, carry)
    second = regroup(mine, others)
    next(second)
    next(second)
    next(ring_first)
    ring_second = gather_over_fac(next(second))
    next(ring_second)
    for hop in range(2, fac_size - 1):
        pieces = next(ring_first)
        next(ring_second)
    head = started(pieces)
    first = finish(*priced(next(ring_first), head), 0)
    next(first)
    next(first)
    pieces = next(ring_second)
    for _ in bits[1:]:
        next(first)
    head = started(pieces)
    next(first)
    second = finish(*priced(next(ring_second), head), 1)
    for _ in range(len(bits) + 1):
        next(second)
    result = next(first)
    next(second)
    return second.send(result)


def solution(mesh):
    in_specs = (P(None, "path", "fac"), P("path", "fac"), P("fac"), P(None, "fac"), P(), P("fac"))
    out_specs = P(None, "path", "fac")
    return jax.shard_map(
        on_device, mesh=mesh, in_specs=in_specs, out_specs=out_specs, check_vma=False
    )
```
